256 devices in a mesh: samp: 32 (over x, z), blk: 8 (over y, core).
Axes of the slice: x: 4, y: 4, z: 8, core: 2. Of those that a mesh axis runs over, the one named last changes fastest.
Arguments:
- genotypes: bfloat16 [262144, 4096], P('samp', 'blk'), may hold values from -20 to 20
- phenotypes: bfloat16 [4, 262144], P(None, 'samp'), may hold values from -8 to 8
Outputs:
- predicted: float32 [4, 262144], P(None, ('samp', 'blk'))
- coefficients: float32 [20, 4096], P(None, 'blk')
The draws below stay inside these ranges and needn't reach their ends.
All inputs are finite; a program needn't handle non-finite values.
Results may differ from the reference program's by a relative error of at most 0.0013.
Values may be sent and summed in bfloat16 or wider, within the bound.
A program may use at most 64 MiB of HBM per device.

```python
import math
import jax
import jax.numpy as jnp
from jax import lax

BLOCK_VARIANTS = 512
TRAIT_COUNT = 4
PENALTY_COUNT = 5
SAMPLE_COUNT = 262144
VARIANTS = 4096


def sample_ramp():
    position = jnp.arange(SAMPLE_COUNT, dtype=jnp.float32) / (SAMPLE_COUNT - 1)
    spread = math.log(3.0) * 0.5
    return jnp.exp(spread * (position - 0.5))


def shared_traits(key):
    trait_key = jax.random.fold_in(key, 7)
    values = jnp.clip(jax.random.normal(trait_key, (TRAIT_COUNT, SAMPLE_COUNT), jnp.float32), -5.0, 5.0)
    return values


def draw_phenotypes(key, part):
    return (shared_traits(key) * sample_ramp()[None, :]).astype(jnp.bfloat16)


def draw_genotypes(key, part):
    traits = shared_traits(key)
    block_count = VARIANTS // BLOCK_VARIANTS
    load_spread = 1.1 / math.sqrt(BLOCK_VARIANTS)
    loadings = jnp.clip(jax.random.normal(jax.random.fold_in(key, 13), (TRAIT_COUNT, VARIANTS), jnp.float32), -3.0, 3.0) * load_spread
    variant_scale = jnp.exp(jax.random.uniform(jax.random.fold_in(key, 17), (VARIANTS,), jnp.float32, math.log(0.5), math.log(2.0)))
    noise_key = jax.random.fold_in(key, 11)
    linkage = 0.97
    renewal = math.sqrt(1.0 - linkage * linkage)

    def innovation(position):
        step_key = jax.random.fold_in(noise_key, position)
        values = jnp.clip(jax.random.normal(step_key, (SAMPLE_COUNT, block_count), jnp.float32), -5.0, 5.0)
        return values

    def advance(state, position):
        state = linkage * state + renewal * innovation(position)
        return (state, state)
    first_state = innovation(jnp.int32(0))
    _, later_states = lax.scan(advance, first_state, jnp.arange(1, BLOCK_VARIANTS, dtype=jnp.int32))
    linked = jnp.concatenate([first_state[None], later_states], axis=0)
    noise_part = jnp.clip(jnp.transpose(linked, (1, 2, 0)).reshape(SAMPLE_COUNT, VARIANTS), -5.0, 5.0)
    combined = noise_part * variant_scale[None, :]
    for trait_index in range(TRAIT_COUNT):
        combined = combined + traits[trait_index][:, None] * loadings[trait_index][None, :]
    combined = jnp.clip(combined * sample_ramp()[:, None], -19.5, 19.5)
    return combined.astype(jnp.bfloat16)


def setup_inputs(seed: int = 0) -> dict:
    key_of = jax.random.split(jax.random.key(seed), 3)
    genotypes = draw_genotypes(jax.random.fold_in(key_of[2], 71), 0)
    phenotypes = draw_phenotypes(jax.random.fold_in(key_of[2], 71), 0)
    return {"genotypes": genotypes, "phenotypes": phenotypes}


ridge_levels = (0.1, 0.4, 1.6, 6.4, 25.6)
level_penalty = 0.5

def solve_level_one(second_level_gram, second_level_cross, count_of_blocks):
    item_count = count_of_blocks * PENALTY_COUNT
    reshaped_array = second_level_gram.reshape(count_of_blocks, TRAIT_COUNT, PENALTY_COUNT, count_of_blocks, TRAIT_COUNT, PENALTY_COUNT)
    diag_part = jnp.diagonal(reshaped_array, axis1=1, axis2=4)
    systems = jnp.transpose(diag_part, (4, 0, 1, 2, 3)).reshape(TRAIT_COUNT, item_count, item_count)
    systems = systems + level_penalty * jnp.eye(item_count, dtype=jnp.float32)[None]
    partial_cross = jnp.diagonal(second_level_cross.reshape(count_of_blocks, TRAIT_COUNT, PENALTY_COUNT, TRAIT_COUNT), axis1=1, axis2=3)
    right_side = jnp.transpose(partial_cross, (2, 0, 1)).reshape(TRAIT_COUNT, item_count, 1)
    cholesky_factor = jnp.linalg.cholesky(systems)
    ridge_weights = jax.scipy.linalg.cho_solve((cholesky_factor, True), right_side)
    return ridge_weights.reshape(TRAIT_COUNT, count_of_blocks, PENALTY_COUNT)

def reference(genotypes, phenotypes):
    count_of_blocks = VARIANTS // BLOCK_VARIANTS
    penalty_values = jnp.array(ridge_levels, dtype=jnp.float32)
    identity_matrix = jnp.eye(BLOCK_VARIANTS, dtype=jnp.float32)
    coef_list = []
    pred_list = []
    for block_index in range(count_of_blocks):
        block_data = genotypes[:, block_index * BLOCK_VARIANTS:(block_index + 1) * BLOCK_VARIANTS]
        gram_matrix = lax.dot_general(block_data.astype(jnp.float32), block_data.astype(jnp.float32), (((0,), (0,)), ((), ())), preferred_element_type=jnp.float32) / SAMPLE_COUNT
        cross_product_matrix = lax.dot_general(block_data.astype(jnp.float32), phenotypes.astype(jnp.float32), (((0,), (1,)), ((), ())), preferred_element_type=jnp.float32) / SAMPLE_COUNT
        systems = gram_matrix[None] + penalty_values[:, None, None] * identity_matrix[None]
        cholesky_factor = jnp.linalg.cholesky(systems)
        solved_system = jax.scipy.linalg.cho_solve((cholesky_factor, True), jnp.broadcast_to(cross_product_matrix, (PENALTY_COUNT, BLOCK_VARIANTS, TRAIT_COUNT)))
        coefficients = jnp.transpose(solved_system, (2, 0, 1)).reshape(TRAIT_COUNT * PENALTY_COUNT, BLOCK_VARIANTS)
        coef_list.append(coefficients)
        preds = lax.dot_general(coefficients.astype(jnp.bfloat16).astype(jnp.float32), block_data.astype(jnp.float32), (((1,), (1,)), ((), ())), preferred_element_type=jnp.float32)
        pred_list.append(preds.astype(jnp.bfloat16))
    every_prediction = jnp.concatenate(pred_list, axis=0)
    second_level_gram = lax.dot_general(every_prediction.astype(jnp.float32), every_prediction.astype(jnp.float32), (((1,), (1,)), ((), ())), preferred_element_type=jnp.float32) / SAMPLE_COUNT
    second_level_cross = lax.dot_general(every_prediction.astype(jnp.float32), phenotypes.astype(jnp.float32), (((1,), (1,)), ((), ())), preferred_element_type=jnp.float32) / SAMPLE_COUNT
    ridge_weights = solve_level_one(second_level_gram, second_level_cross, count_of_blocks)
    reshaped_predictions = every_prediction.reshape(count_of_blocks, TRAIT_COUNT, PENALTY_COUNT, SAMPLE_COUNT).astype(jnp.float32)
    predicted = jnp.einsum('tbk,btks->ts', ridge_weights, reshaped_predictions, precision=lax.Precision.HIGHEST)
    return (predicted, jnp.concatenate(coef_list, axis=1))
```

```python
import jax
import jax.numpy as jnp
from jax import lax
from jax.experimental import pallas as pl
from jax.experimental.pallas import tpu as pltpu
from jax.sharding import PartitionSpec as P

TRAITS = 4
PENALTIES = 5
SAMPLES = 262144
BLOCK = 512
XS, ZS, BLKS = 4, 8, 8
ridge_levels = (0.1, 0.4, 1.6, 6.4, 25.6)
level_penalty = 0.5

ROWS = SAMPLES // (XS * ZS)
PART = ROWS // BLKS
F32 = jnp.float32
BF16 = jnp.bfloat16
HI = lax.Precision.HIGHEST
NT = (((1,), (1,)), ((), ()))
NN = (((1,), (0,)), ((), ()))
MESH = pl.DeviceIdType.MESH
VMEM = pltpu.VMEM

CHUNK = 2048
A_ROWS = 1024
B_ROWS = 512
PACKED = A_ROWS + B_ROWS


def place():
    samp = lax.axis_index("samp")
    return lax.div(samp, ZS), lax.rem(samp, ZS)


def along_x(x, z, step):
    other = lax.rem(x + step, XS)
    return other, {"samp": other * ZS + z}


def along_z(x, z, step):
    other = lax.rem(z + step, ZS)
    return other, {"samp": x * ZS + other}


def rows_at(index, size):
    return pl.ds(pl.multiple_of(index * size, size), size)


def send(src, dst, sems, slot, device):
    copy = pltpu.make_async_remote_copy(
        src_ref=src, dst_ref=dst, send_sem=sems.at[0, slot], recv_sem=sems.at[1, slot],
        device_id=device, device_id_type=MESH)
    copy.start()
    return copy


def finish(copies):
    for copy in copies:
        copy.wait()


def gram_sum_kernel(x_hbm, ph_ref, out_ref, xbuf, left, right, acc, ax, axs, az, azs, bz, bzs, bx, bxs,
                    load_sem, axr, azr, bzr, bxr, axg, azg, bzg, bxg):
    x, z = place()
    chunks = ROWS // CHUNK
    for c in range(chunks):
        pltpu.make_async_copy(x_hbm.at[pl.ds(c * CHUNK, CHUNK)], xbuf.at[pl.ds(c * CHUNK, CHUNK)], load_sem.at[c]).start()
    barrier = pltpu.get_barrier_semaphore()
    for step in range(1, XS):
        pl.semaphore_signal(barrier, inc=1, device_id=along_x(x, z, step)[1], device_id_type=MESH)
    for step in range(1, ZS):
        pl.semaphore_signal(barrier, inc=1, device_id=along_z(x, z, step)[1], device_id_type=MESH)

    left[...] = jnp.zeros_like(left)
    right[...] = jnp.zeros_like(right)
    for c in range(chunks):
        span = pl.ds(c * CHUNK, CHUNK)
        pltpu.make_async_copy(x_hbm.at[span], xbuf.at[span], load_sem.at[c]).wait()
        values = xbuf[span, :]
        flipped = jnp.concatenate([values.T, ph_ref[:, span], jnp.zeros((12, CHUNK), BF16)], 0)
        left[...] += lax.dot_general(flipped, values[:, :256], NN, preferred_element_type=F32)
        right[...] += lax.dot_general(flipped[256:], values[:, 256:], NN, preferred_element_type=F32)

    acc[0:512, :] = left[0:512, 0:128]
    acc[512:896, :] = left[128:512, 128:256]
    acc[896:1152, :] = right[0:256, 0:128]
    acc[1152:1280, :] = right[128:256, 128:256]
    acc[1280:1288, :] = jnp.concatenate([left[512:516, 0:128], left[512:516, 128:256]], 0)
    acc[1288:1296, :] = jnp.concatenate([right[256:260, 0:128], right[256:260, 128:256]], 0)
    acc[1296:PACKED, :] = jnp.zeros((PACKED - 1296, 128), F32)

    pl.semaphore_wait(barrier, XS - 1 + ZS - 1)
    a_out, b_out = [], []
    for step in range(1, ZS):
        other, device = along_z(x, z, step)
        src = acc.at[pl.ds(pl.multiple_of(A_ROWS + other * 64, 64), 64)]
        b_out.append(send(src, bz.at[step - 1], bzr, step - 1, device))
    for step in range(1, XS):
        other, device = along_x(x, z, step)
        a_out.append(send(acc.at[rows_at(other, 256)], ax.at[step - 1], axr, step - 1, device))
    finish(b_out)
    total = acc[pl.ds(pl.multiple_of(A_ROWS + z * 64, 64), 64), :]
    for i in range(ZS - 1):
        total = total + bz[i]
    bzs[...] = total
    b_out = []
    for step in range(1, XS):
        other, device = along_x(x, z, step)
        b_out.append(send(bzs.at[rows_at(other, 16)], bx.at[step - 1], bxr, step - 1, device))
    finish(a_out)
    total = acc[rows_at(x, 256), :]
    for i in range(XS - 1):
        total = total + ax[i]
    axs[...] = total
    a_out = []
    for step in range(1, ZS):
        other, device = along_z(x, z, step)
        a_out.append(send(axs.at[rows_at(other, 32)], az.at[step - 1], azr, step - 1, device))
    finish(b_out)
    total = bzs[rows_at(x, 16), :]
    for i in range(XS - 1):
        total = total + bx[i]
    bxs[rows_at(x, 16), :] = total
    b_out = []
    for step in range(1, XS):
        _, device = along_x(x, z, step)
        b_out.append(send(bxs.at[rows_at(x, 16)], bxs.at[rows_at(x, 16)], bxg, step - 1, device))
    finish(a_out)
    total = axs[rows_at(z, 32), :]
    for i in range(ZS - 1):
        total = total + az[i]
    azs[rows_at(z, 32), :] = total
    a_out = []
    for step in range(1, ZS):
        _, device = along_z(x, z, step)
        a_out.append(send(azs.at[rows_at(z, 32)], azs.at[rows_at(z, 32)], azg, step - 1, device))
    finish(b_out)
    out_ref[pl.ds(pl.multiple_of(A_ROWS + z * 64, 64), 64), :] = bxs[...]
    b_out = []
    for step in range(1, ZS):
        _, device = along_z(x, z, step)
        span = pl.ds(pl.multiple_of(A_ROWS + z * 64, 64), 64)
        b_out.append(send(bxs, out_ref.at[span], bzg, step - 1, device))
    finish(a_out)
    out_ref[rows_at(x, 256), :] = azs[...]
    a_out = []
    for step in range(1, XS):
        _, device = along_x(x, z, step)
        a_out.append(send(azs, out_ref.at[rows_at(x, 256)], axg, step - 1, device))
    finish(b_out)
    finish(a_out)


def dma(n):
    return pltpu.SemaphoreType.DMA((2, n))


def gram_sum(genotypes, phenotypes):
    x1, z1 = XS - 1, ZS - 1
    return pl.pallas_call(
        gram_sum_kernel,
        out_shape=jax.ShapeDtypeStruct((PACKED, 128), F32),
        in_specs=[pl.BlockSpec(memory_space=pl.ANY), pl.BlockSpec(memory_space=VMEM)],
        out_specs=pl.BlockSpec(memory_space=VMEM),
        scratch_shapes=[
            VMEM((ROWS, BLOCK), BF16), VMEM((528, 256), F32), VMEM((272, 256), F32), VMEM((PACKED, 128), F32),
            VMEM((x1, 256, 128), F32), VMEM((256, 128), F32), VMEM((z1, 32, 128), F32), VMEM((256, 128), F32),
            VMEM((z1, 64, 128), F32), VMEM((64, 128), F32), VMEM((x1, 16, 128), F32), VMEM((64, 128), F32),
            pltpu.SemaphoreType.DMA((ROWS // CHUNK,)),
            dma(x1), dma(z1), dma(z1), dma(x1), dma(x1), dma(z1), dma(z1), dma(x1),
        ],
        compiler_params=pltpu.CompilerParams(
            collective_id=0, has_side_effects=True, vmem_limit_bytes=40 << 20),
        name="gram_sum",
    )(genotypes, phenotypes)


def recip(d):
    r = pl.reciprocal(d, approx=True)
    r = r * (2.0 - d * r)
    r = r * (2.0 - d * r)
    return r


def tree(terms):
    while len(terms) > 1:
        terms = [terms[i] + terms[i + 1] for i in range(0, len(terms), 2)]
    return terms[0]


def sweep(rows, t, lane, sub):
    lo = 8 * t
    inside = (lane >= lo) & (lane < lo + 8)
    pivot_rows = rows[t]
    cols = [jnp.broadcast_to(pivot_rows[:, lo + j:lo + j + 1], (8, 128)) for j in range(8)]
    kept = jnp.where(inside, jnp.where(lane == sub + lo, 1.0, 0.0), pivot_rows)
    for p in range(8):
        col = cols[p]
        row = [jnp.broadcast_to(cols[j][p:p + 1, :], (8, 128)) for j in range(8)]
        r = recip(row[p])
        cols = [
            jnp.where(sub == p, r, -col * r) if j == p
            else jnp.where(sub == p, row[j] * r, cols[j] - (col * row[j]) * r)
            for j in range(8)
        ]
    new = tree([cols[j] * jnp.broadcast_to(kept[j:j + 1, :], (8, 128)) for j in range(8)])
    spread = [jnp.broadcast_to(new[j:j + 1, :], (8, 128)) for j in range(8)]
    out = []
    for i, group in enumerate(rows):
        if i == t:
            out.append(new)
        else:
            q = [jnp.broadcast_to(group[:, lo + j:lo + j + 1], (8, 128)) for j in range(8)]
            out.append(jnp.where(inside, 0.0, group) - tree([q[j] * spread[j] for j in range(8)]))
    return out


def iotas():
    shape = (8, 128)
    return lax.broadcasted_iota(jnp.int32, shape, 1), lax.broadcasted_iota(jnp.int32, shape, 0)


def solve0_kernel(g_ref, x_ref, a_ref, w_ref, inv_ref):
    lane, sub = iotas()
    _, z = place()
    which = lax.rem(z, PENALTIES)
    penalty = jnp.float32(ridge_levels[0])
    for k in range(1, PENALTIES):
        penalty = jnp.where(which == k, jnp.float32(ridge_levels[k]), penalty)
    base = (0, 512, 896, 1152)
    off = (0, 520, 912, 1176)
    for k in range(4):
        n = 512 - 128 * k
        a_ref[off[k]:off[k] + n, :] = g_ref[base[k]:base[k] + n, :] / SAMPLES
        cross = g_ref[1280 + 4 * k:1284 + 4 * k, :] / SAMPLES
        a_ref[off[k] + n:off[k] + n + 8, :] = jnp.concatenate([cross, jnp.zeros((4, 128), F32)], 0)
    for k in range(4):
        n = 512 - 128 * k
        rows = [a_ref[off[k] + 8 * i:off[k] + 8 * i + 8, :] + jnp.where(lane == sub + 8 * i, penalty, 0.0)
                for i in range(16)]
        for t in range(16):
            rows = sweep(rows, t, lane, sub)
        for i in range(16):
            inv_ref[8 * i:8 * i + 8, :] = rows[i]
        panel = a_ref[off[k] + 128:off[k] + n + 8, :]
        w = lax.dot_general(panel, inv_ref[...], NN, precision=HI, preferred_element_type=F32)
        w_ref[off[k]:off[k] + n - 120, :] = w
        for j in range(k + 1, 4):
            skip = 128 * (j - k - 1)
            change = lax.dot_general(panel[skip:, :], w[skip:skip + 128, :], NT, precision=HI, preferred_element_type=F32)
            a_ref[off[j]:off[j] + 520 - 128 * j, :] -= change
    parts = [None] * 4
    for k in (3, 2, 1, 0):
        n = 512 - 128 * k
        y = w_ref[off[k] + n - 128:off[k] + n - 120, :]
        if k < 3:
            later = jnp.concatenate(parts[k + 1:], 1)
            y = y - lax.dot_general(later, w_ref[off[k]:off[k] + n - 128, :], NN, precision=HI, preferred_element_type=F32)
        parts[k] = y
    x_ref[...] = jnp.concatenate(parts, 1)


def solve0(sums):
    return pl.pallas_call(
        solve0_kernel,
        out_shape=jax.ShapeDtypeStruct((8, BLOCK), F32),
        in_specs=[pl.BlockSpec(memory_space=VMEM)],
        out_specs=pl.BlockSpec(memory_space=VMEM),
        scratch_shapes=[VMEM((1312, 128), F32), VMEM((1312, 128), F32), VMEM((128, 128), F32)],
        name="solve0",
    )(sums)


def level1_kernel(beta_ref, ph_ref, x_hbm, pred_ref, coef_ref, xbuf, betas, low, stage, pall, lg, ly, lc, lx, lz, ls, wt, wts,
                  load_sem, bsem, psem, ysem, csem, xsem, zsem, wsem):
    x, z = place()
    blk = lax.axis_index("blk")
    y, core = lax.div(blk, 2), lax.rem(blk, 2)
    lane, sub = iotas()
    for c in range(BLKS):
        pltpu.make_async_copy(x_hbm.at[pl.ds(c * PART, PART)], xbuf.at[pl.ds(c * PART, PART)], load_sem.at[c]).start()
    barrier = pltpu.get_barrier_semaphore()
    for step in range(1, XS):
        pl.semaphore_signal(barrier, inc=1, device_id=along_x(x, z, step)[1], device_id_type=MESH)
    for step in range(1, ZS):
        pl.semaphore_signal(barrier, inc=1, device_id=along_z(x, z, step)[1], device_id_type=MESH)
    for step in range(1, BLKS):
        pl.semaphore_signal(barrier, inc=1, device_id={"blk": lax.rem(blk + step, BLKS)}, device_id_type=MESH)
    for c in range(BLKS):
        pltpu.make_async_copy(x_hbm.at[pl.ds(c * PART, PART)], xbuf.at[pl.ds(c * PART, PART)], load_sem.at[c]).wait()
    pl.semaphore_wait(barrier, XS + ZS + BLKS - 3)

    def to(k, other):
        return pltpu.make_async_remote_copy(
            src_ref=beta_ref, dst_ref=betas.at[k], send_sem=bsem.at[0, other], recv_sem=bsem.at[1, k],
            device_id={"samp": x * ZS + other}, device_id_type=MESH)

    for k in range(PENALTIES):
        @pl.when(z == k)
        def _():
            for step in range(1, ZS):
                to(k, (k + step) % ZS).start()
            betas[k] = beta_ref[...]
    for k in range(PENALTIES):
        @pl.when(z == k)
        def _():
            for step in range(1, ZS):
                to(k, (k + step) % ZS).wait_send()

        @pl.when(z != k)
        def _():
            to(k, 0).wait_recv()
    groups = []
    for t in range(TRAITS):
        groups.append(jnp.concatenate([betas[k][t:t + 1, :] for k in range(PENALTIES)], 0))
    coef_ref[...] = jnp.concatenate(groups, 0)
    blank = jnp.zeros((8 - PENALTIES, BLOCK), F32)
    low[...] = jnp.concatenate([v for g in groups for v in (g, blank)], 0).astype(BF16)

    def predict(owner):
        part = xbuf[rows_at(owner, PART), :]
        return lax.dot_general(low[...], part, NT, preferred_element_type=F32).astype(BF16)

    def part_copy(step):
        owner = lax.rem(blk + step, BLKS)
        return pltpu.make_async_remote_copy(
            src_ref=stage.at[step], dst_ref=pall.at[blk], send_sem=psem.at[0, step], recv_sem=psem.at[1, step],
            device_id={"blk": owner}, device_id_type=MESH)

    def emit(step, carry):
        stage[step] = predict(lax.rem(blk + step, BLKS))
        part_copy(step).start()
        return carry

    lax.fori_loop(1, BLKS, emit, 0)
    pall[blk] = predict(blk)

    def landed(step, carry):
        part_copy(step).wait()
        return carry

    lax.fori_loop(1, BLKS, landed, 0)

    preds = pall[...].astype(F32)
    own = ph_ref[:, rows_at(blk, PART)]
    tail = jnp.concatenate([own, jnp.zeros((12, PART), BF16)], 0)
    by_trait = []
    for t in range(TRAITS):
        pt = preds[:, 8 * t:8 * t + 8, :].reshape(64, PART).astype(BF16)
        by_trait.append(pt)
        sums = lax.dot_general(jnp.concatenate([pt, tail], 0), pt, NT, preferred_element_type=F32)
        lg[t, 0:32, :] = jnp.concatenate([sums[0:32], sums[32:64]], 1)
        lg[t, 32:40, :] = jnp.concatenate([sums[64:72], jnp.zeros((8, 64), F32)], 1)
    copies = []
    for step in range(1, 4):
        other = lax.rem(y + step, 4)
        copies.append(send(lg.at[other], ly.at[step - 1], ysem, step - 1, {"blk": other * 2 + core}))
    finish(copies)
    total = lg[y]
    for i in range(3):
        total = total + ly[i]
    ls[0] = total
    finish([send(ls.at[0], lc, csem, 0, {"blk": y * 2 + 1 - core})])
    ls[1] = total + lc[...]
    copies = []
    for step in range(1, XS):
        copies.append(send(ls.at[1], lx.at[step - 1], xsem, step - 1, along_x(x, z, step)[1]))
    finish(copies)
    total = ls[1]
    for i in range(XS - 1):
        total = total + lx[i]
    ls[2] = total
    copies = []
    for step in range(1, ZS):
        copies.append(send(ls.at[2], lz.at[step - 1], zsem, step - 1, along_z(x, z, step)[1]))
    finish(copies)
    total = ls[2]
    for i in range(ZS - 1):
        total = total + lz[i]
    total = total / SAMPLES
    blank = jnp.zeros((32, 64), F32)
    full = jnp.concatenate([
        jnp.concatenate([total[0:32, 0:64], blank], 1),
        jnp.concatenate([total[0:32, 64:128], blank], 1),
        total[32:40]], 0)
    rows = [full[8 * i:8 * i + 8] + (jnp.where(lane == sub + 8 * i, level_penalty, 0.0) if i < 8 else 0.0) for i in range(9)]
    for t in range(8):
        rows = sweep(rows, t, lane, sub)
    mine = jnp.where(sub == y, -rows[8], 0.0)
    wt[...] = mine
    copies = []
    for step in range(1, 4):
        other = lax.rem(y + step, 4)
        copies.append(send(wt, wts.at[step - 1], wsem, step - 1, {"blk": other * 2 + core}))
    finish(copies)
    weights = mine + wts[0] + wts[1] + wts[2]
    wide = jnp.concatenate([jnp.where(sub == t, weights, 0.0)[:, 0:64] for t in range(TRAITS)], 1)
    w1 = wide.astype(BF16).astype(F32)
    w2 = (wide - w1).astype(BF16).astype(F32)
    w3 = wide - w1 - w2
    parts = jnp.concatenate([w1, w2, w3, jnp.zeros((8, 256), F32)], 0).astype(BF16)
    terms = lax.dot_general(parts, jnp.concatenate(by_trait, 0), NN, preferred_element_type=F32)
    pred_ref[...] = (terms[0:8] + terms[8:16] + terms[16:24])[0:4]


def level1(beta, phenotypes, genotypes):
    return pl.pallas_call(
        level1_kernel,
        out_shape=(jax.ShapeDtypeStruct((TRAITS, PART), F32), jax.ShapeDtypeStruct((TRAITS * PENALTIES, BLOCK), F32)),
        in_specs=[pl.BlockSpec(memory_space=VMEM), pl.BlockSpec(memory_space=VMEM), pl.BlockSpec(memory_space=pl.ANY)],
        out_specs=(pl.BlockSpec(memory_space=VMEM),) * 2,
        scratch_shapes=[
            VMEM((ROWS, BLOCK), BF16), VMEM((PENALTIES, 8, BLOCK), F32), VMEM((32, BLOCK), BF16),
            VMEM((BLKS, 32, PART), BF16), VMEM((BLKS, 32, PART), BF16),
            VMEM((4, 40, 128), F32), VMEM((3, 40, 128), F32), VMEM((40, 128), F32), VMEM((XS - 1, 40, 128), F32),
            VMEM((ZS - 1, 40, 128), F32), VMEM((3, 40, 128), F32), VMEM((8, 128), F32), VMEM((3, 8, 128), F32),
            pltpu.SemaphoreType.DMA((BLKS,)),
            dma(ZS), dma(BLKS), dma(3), dma(1), dma(XS - 1), dma(ZS - 1), dma(3),
        ],
        compiler_params=pltpu.CompilerParams(
            collective_id=1, has_side_effects=True, vmem_limit_bytes=40 << 20),
        name="level1",
    )(beta, phenotypes, genotypes)


def local(genotypes, phenotypes):
    sums = gram_sum(genotypes, phenotypes)
    beta = solve0(sums)
    return level1(beta, phenotypes, genotypes)


def solution(mesh):
    return jax.shard_map(
        local,
        mesh=mesh,
        in_specs=(P("samp", "blk"), P(None, "samp")),
        out_specs=(P(None, ("samp", "blk")), P(None, "blk")),
        check_vma=False,
    )
```

```python
import jax
import jax.numpy as jnp
from jax import lax
from jax.experimental import pallas as pl
from jax.experimental.pallas import tpu as pltpu
from jax.sharding import PartitionSpec as P

TRAITS = 4
PENALTIES = 5
SAMPLES = 262144
BLOCK = 512
XS, ZS, BLKS = 4, 8, 8
ridge_levels = (0.1, 0.4, 1.6, 6.4, 25.6)
level_penalty = 0.5

ROWS = SAMPLES // (XS * ZS)
PART = ROWS // BLKS
F32 = jnp.float32
BF16 = jnp.bfloat16
HI = lax.Precision.HIGHEST
NT = (((1,), (1,)), ((), ()))
NN = (((1,), (0,)), ((), ()))
MESH = pl.DeviceIdType.MESH
VMEM = pltpu.VMEM

CHUNK = 2048
A_ROWS = 1024
B_ROWS = 256
PACKED = A_ROWS + B_ROWS
OWNED = 40
USED = 1168
BELOW = {(1, 0): 0, (2, 0): 128, (3, 0): 256, (2, 1): 384, (3, 1): 512, (3, 2): 640}
TOP, CORNER, CROSS = 768, 1024, 1152

SOLVERS = ((0, 13), (9, 22), (18, 31), (27, 16), (4, 2))


def place():
    samp = lax.axis_index("samp")
    return lax.div(samp, ZS), lax.rem(samp, ZS)


def solver_of(k, core):
    first, second = SOLVERS[k]
    return first + core * (second - first)


def solves(samp, core):
    count = jnp.int32(0)
    for k in range(PENALTIES):
        count = count + jnp.where(samp == solver_of(k, core), jnp.int32(1), jnp.int32(0))
    return count


def along_x(x, z, step):
    other = lax.rem(x + step, XS)
    return other, {"samp": other * ZS + z}


def along_z(x, z, step):
    other = lax.rem(z + step, ZS)
    return other, {"samp": x * ZS + other}


def rows_at(index, size):
    return pl.ds(pl.multiple_of(index * size, size), size)


def send(src, dst, sems, slot, device):
    copy = pltpu.make_async_remote_copy(
        src_ref=src, dst_ref=dst, send_sem=sems.at[0, slot], recv_sem=sems.at[1, slot],
        device_id=device, device_id_type=MESH)
    copy.start()
    return copy


def finish(copies):
    for copy in copies:
        copy.wait()


def gram_sum_kernel(x_hbm, ph_ref, out_ref, xbuf, left, right, acc, ax, axs, az, bz, bzs, bx, mine,
                    load_sem, axr, azr, bzr, bxr, out_sem, in_sem):
    x, z = place()
    samp = lax.axis_index("samp")
    core = lax.rem(lax.axis_index("blk"), 2)
    chunks = ROWS // CHUNK
    for c in range(chunks):
        pltpu.make_async_copy(x_hbm.at[pl.ds(c * CHUNK, CHUNK)], xbuf.at[pl.ds(c * CHUNK, CHUNK)], load_sem.at[c]).start()
    barrier = pltpu.get_barrier_semaphore()
    for step in range(1, XS):
        pl.semaphore_signal(barrier, inc=1, device_id=along_x(x, z, step)[1], device_id_type=MESH)
    for step in range(1, ZS):
        pl.semaphore_signal(barrier, inc=1, device_id=along_z(x, z, step)[1], device_id_type=MESH)
    for k in range(PENALTIES):
        @pl.when(samp == solver_of(k, core))
        def _():
            def greet(step, carry):
                other = lax.rem(samp + step, XS * ZS)
                pl.semaphore_signal(barrier, inc=1, device_id={"samp": other}, device_id_type=MESH)
                return carry

            lax.fori_loop(1, XS * ZS, greet, 0)

    left[...] = jnp.zeros_like(left)
    right[...] = jnp.zeros_like(right)
    for c in range(chunks):
        span = pl.ds(c * CHUNK, CHUNK)
        pltpu.make_async_copy(x_hbm.at[span], xbuf.at[span], load_sem.at[c]).wait()
        values = xbuf[span, :]
        flipped = jnp.concatenate([values.T, ph_ref[:, span], jnp.zeros((12, CHUNK), BF16)], 0)
        left[...] += lax.dot_general(flipped, values[:, :256], NN, preferred_element_type=F32)
        right[...] += lax.dot_general(flipped[256:], values[:, 256:], NN, preferred_element_type=F32)

    def block(i, j, top=0, size=128):
        if j < 2:
            return left[128 * i + top:128 * i + top + size, 128 * j:128 * j + 128]
        return right[128 * i - 256 + top:128 * i - 256 + top + size, 128 * j - 256:128 * j - 128]

    for (i, j), row in BELOW.items():
        acc[row:row + 128, :] = block(i, j)
    for k in range(4):
        acc[TOP + 64 * k:TOP + 64 * k + 64, :] = block(k, k, 0, 64)
    for k in range(2):
        acc[CORNER + 64 * k:CORNER + 64 * k + 64, :] = jnp.concatenate(
            [block(2 * k, 2 * k, 64, 64)[:, 64:], block(2 * k + 1, 2 * k + 1, 64, 64)[:, 64:]], 1)
    acc[CROSS:CROSS + 8, :] = jnp.concatenate([left[512:516, 0:128], left[512:516, 128:256]], 0)
    acc[CROSS + 8:CROSS + 16, :] = jnp.concatenate([right[256:260, 0:128], right[256:260, 128:256]], 0)
    acc[USED:PACKED, :] = jnp.zeros((PACKED - USED, 128), F32)

    def b_rows(index):
        return pl.ds(pl.multiple_of(A_ROWS + index * 32, 32), 32)

    pl.semaphore_wait(barrier, XS + ZS - 2 + PENALTIES - solves(samp, core))
    a_out, b_out = [], []
    for step in range(1, ZS):
        other, device = along_z(x, z, step)
        b_out.append(send(acc.at[b_rows(other)], bz.at[step - 1], bzr, step - 1, device))
    for step in range(1, XS):
        other, device = along_x(x, z, step)
        a_out.append(send(acc.at[rows_at(other, 256)], ax.at[step - 1], axr, step - 1, device))
    finish(a_out)
    total = acc[rows_at(x, 256), :]
    for i in range(XS - 1):
        total = total + ax[i]
    axs[...] = total
    a_out = []
    for step in range(1, ZS):
        other, device = along_z(x, z, step)
        a_out.append(send(axs.at[rows_at(other, 32)], az.at[step - 1], azr, step - 1, device))
    finish(b_out)
    total = acc[b_rows(z), :]
    for i in range(ZS - 1):
        total = total + bz[i]
    bzs[...] = total
    b_out = []
    for step in range(1, XS):
        other, device = along_x(x, z, step)
        b_out.append(send(bzs.at[rows_at(other, 8)], bx.at[step - 1], bxr, step - 1, device))
    finish(b_out)
    total = bzs[rows_at(x, 8), :]
    for i in range(XS - 1):
        total = total + bx[i]
    mine[32:40, :] = total
    finish(a_out)
    total = axs[rows_at(z, 32), :]
    for i in range(ZS - 1):
        total = total + az[i]
    mine[0:32, :] = total

    def to(k, source):
        return pltpu.make_async_remote_copy(
            src_ref=mine, dst_ref=out_ref.at[rows_at(source, OWNED)], send_sem=out_sem.at[k], recv_sem=in_sem.at[source],
            device_id={"samp": solver_of(k, core)}, device_id_type=MESH)

    for k in range(PENALTIES):
        @pl.when(samp != solver_of(k, core))
        def _():
            to(k, samp).start()
    for k in range(PENALTIES):
        @pl.when(samp == solver_of(k, core))
        def _():
            out_ref[rows_at(samp, OWNED), :] = mine[...]

            def take(step, carry):
                to(k, lax.rem(samp + step, XS * ZS)).wait_recv()
                return carry

            lax.fori_loop(1, XS * ZS, take, 0)
    for k in range(PENALTIES):
        @pl.when(samp != solver_of(k, core))
        def _():
            to(k, samp).wait_send()


def dma(n):
    return pltpu.SemaphoreType.DMA((2, n))


def gram_sum(genotypes, phenotypes):
    x1, z1 = XS - 1, ZS - 1
    return pl.pallas_call(
        gram_sum_kernel,
        out_shape=jax.ShapeDtypeStruct((PACKED, 128), F32),
        in_specs=[pl.BlockSpec(memory_space=pl.ANY), pl.BlockSpec(memory_space=VMEM)],
        out_specs=pl.BlockSpec(memory_space=VMEM),
        scratch_shapes=[
            VMEM((ROWS, BLOCK), BF16), VMEM((528, 256), F32), VMEM((272, 256), F32), VMEM((PACKED, 128), F32),
            VMEM((x1, 256, 128), F32), VMEM((256, 128), F32), VMEM((z1, 32, 128), F32),
            VMEM((z1, 32, 128), F32), VMEM((32, 128), F32), VMEM((x1, 8, 128), F32), VMEM((OWNED, 128), F32),
            pltpu.SemaphoreType.DMA((ROWS // CHUNK,)),
            dma(x1), dma(z1), dma(z1), dma(x1), pltpu.SemaphoreType.DMA((PENALTIES,)), pltpu.SemaphoreType.DMA((XS * ZS,)),
        ],
        compiler_params=pltpu.CompilerParams(
            collective_id=0, has_side_effects=True, vmem_limit_bytes=57 << 20),
        name="gram_sum",
    )(genotypes, phenotypes)


def recip(d):
    r = pl.reciprocal(d, approx=True)
    r = r * (2.0 - d * r)
    r = r * (2.0 - d * r)
    return r


def tree(terms):
    while len(terms) > 1:
        terms = [terms[i] + terms[i + 1] for i in range(0, len(terms), 2)]
    return terms[0]


def sweep(rows, t, lane, sub):
    lo = 8 * t
    inside = (lane >= lo) & (lane < lo + 8)
    pivot_rows = rows[t]
    cols = [jnp.broadcast_to(pivot_rows[:, lo + j:lo + j + 1], (8, 128)) for j in range(8)]
    kept = jnp.where(inside, jnp.where(lane == sub + lo, 1.0, 0.0), pivot_rows)
    for p in range(8):
        col = cols[p]
        row = [jnp.broadcast_to(cols[j][p:p + 1, :], (8, 128)) for j in range(8)]
        r = recip(row[p])
        cols = [
            jnp.where(sub == p, r, -col * r) if j == p
            else jnp.where(sub == p, row[j] * r, cols[j] - (col * row[j]) * r)
            for j in range(8)
        ]
    new = tree([cols[j] * jnp.broadcast_to(kept[j:j + 1, :], (8, 128)) for j in range(8)])
    spread = [jnp.broadcast_to(new[j:j + 1, :], (8, 128)) for j in range(8)]
    out = []
    for i, group in enumerate(rows):
        if i == t:
            out.append(new)
        else:
            q = [jnp.broadcast_to(group[:, lo + j:lo + j + 1], (8, 128)) for j in range(8)]
            out.append(jnp.where(inside, 0.0, group) - tree([q[j] * spread[j] for j in range(8)]))
    return out


def iotas():
    shape = (8, 128)
    return lax.broadcasted_iota(jnp.int32, shape, 1), lax.broadcasted_iota(jnp.int32, shape, 0)


def solve0_kernel(g_ref, x_ref, a_ref, w_ref, inv_ref):
    lane, sub = iotas()
    samp = lax.axis_index("samp")
    core = lax.rem(lax.axis_index("blk"), 2)
    penalty = jnp.float32(ridge_levels[0])
    for k in range(1, PENALTIES):
        penalty = jnp.where(samp == solver_of(k, core), jnp.float32(ridge_levels[k]), penalty)

    def packed(row, count):
        pieces = []
        while count:
            if row < A_ROWS:
                owner, skip = row // 32, row % 32
                size = min(32 - skip, count)
                start = OWNED * owner + skip
            else:
                owner, skip = ((row - A_ROWS) % 32) // 8 * ZS + (row - A_ROWS) // 32, row % 8
                size = min(8 - skip, count)
                start = OWNED * owner + 32 + skip
            pieces.append(g_ref[start:start + size, :])
            row, count = row + size, count - size
        return (jnp.concatenate(pieces, 0) if len(pieces) > 1 else pieces[0]) / SAMPLES

    off = (0, 520, 912, 1176)
    for k in range(4):
        n = 512 - 128 * k
        upper = packed(TOP + 64 * k, 64)
        corner = packed(CORNER + 64 * (k // 2), 64)[:, 64 * (k % 2):64 * (k % 2) + 64]
        a_ref[off[k]:off[k] + 64, :] = upper
        a_ref[off[k] + 64:off[k] + 128, :] = jnp.concatenate([upper[:, 64:].T, corner], 1)
        for i in range(k + 1, 4):
            row = off[k] + 128 * (i - k)
            a_ref[row:row + 128, :] = packed(BELOW[i, k], 128)
        cross = packed(CROSS + 4 * k, 4)
        a_ref[off[k] + n:off[k] + n + 8, :] = jnp.concatenate([cross, jnp.zeros((4, 128), F32)], 0)
    for k in range(4):
        n = 512 - 128 * k
        rows = [a_ref[off[k] + 8 * i:off[k] + 8 * i + 8, :] + jnp.where(lane == sub + 8 * i, penalty, 0.0)
                for i in range(16)]
        for t in range(16):
            rows = sweep(rows, t, lane, sub)
        for i in range(16):
            inv_ref[8 * i:8 * i + 8, :] = rows[i]
        panel = a_ref[off[k] + 128:off[k] + n + 8, :]
        w = lax.dot_general(panel, inv_ref[...], NN, precision=HI, preferred_element_type=F32)
        w_ref[off[k]:off[k] + n - 120, :] = w
        for j in range(k + 1, 4):
            skip = 128 * (j - k - 1)
            change = lax.dot_general(panel[skip:, :], w[skip:skip + 128, :], NT, precision=HI, preferred_element_type=F32)
            a_ref[off[j]:off[j] + 520 - 128 * j, :] -= change
    parts = [None] * 4
    for k in (3, 2, 1, 0):
        n = 512 - 128 * k
        y = w_ref[off[k] + n - 128:off[k] + n - 120, :]
        if k < 3:
            later = jnp.concatenate(parts[k + 1:], 1)
            y = y - lax.dot_general(later, w_ref[off[k]:off[k] + n - 128, :], NN, precision=HI, preferred_element_type=F32)
        parts[k] = y
    x_ref[...] = jnp.concatenate([part[0:TRAITS] for part in parts], 0)


def solve0(sums):
    return pl.pallas_call(
        solve0_kernel,
        out_shape=jax.ShapeDtypeStruct((4 * TRAITS, 128), F32),
        in_specs=[pl.BlockSpec(memory_space=VMEM)],
        out_specs=pl.BlockSpec(memory_space=VMEM),
        scratch_shapes=[VMEM((1312, 128), F32), VMEM((1312, 128), F32), VMEM((128, 128), F32)],
        name="solve0",
    )(sums)


def level1_kernel(beta_ref, ph_ref, x_hbm, pred_ref, coef_ref, xbuf, betas, wide_low, stage, pall, lg, ly, lx, lz, ls, wt, wts,
                  load_sem, bsem, bget, psem, ysem, xsem, zsem, wsem):
    x, z = place()
    blk = lax.axis_index("blk")
    y, core = lax.div(blk, 2), lax.rem(blk, 2)
    lane, sub = iotas()
    for c in range(BLKS):
        pltpu.make_async_copy(x_hbm.at[pl.ds(c * PART, PART)], xbuf.at[pl.ds(c * PART, PART)], load_sem.at[c]).start()
    barrier = pltpu.get_barrier_semaphore()
    for step in range(1, XS):
        pl.semaphore_signal(barrier, inc=1, device_id=along_x(x, z, step)[1], device_id_type=MESH)
    for step in range(1, ZS):
        pl.semaphore_signal(barrier, inc=1, device_id=along_z(x, z, step)[1], device_id_type=MESH)
    for step in range(1, BLKS):
        pl.semaphore_signal(barrier, inc=1, device_id={"blk": lax.rem(blk + step, BLKS)}, device_id_type=MESH)
    samp = lax.axis_index("samp")
    for k in range(PENALTIES):
        @pl.when(samp != solver_of(k, core))
        def _():
            pl.semaphore_signal(barrier, inc=1, device_id={"samp": solver_of(k, core)}, device_id_type=MESH)
    pl.semaphore_wait(barrier, XS + ZS + BLKS - 3 + (XS * ZS - 1) * solves(samp, core))

    def to(k, step):
        other = lax.rem(solver_of(k, core) + step, XS * ZS)
        return pltpu.make_async_remote_copy(
            src_ref=beta_ref, dst_ref=betas.at[k], send_sem=bsem.at[step], recv_sem=bget.at[k],
            device_id={"samp": other}, device_id_type=MESH)

    for k in range(PENALTIES):
        @pl.when(samp == solver_of(k, core))
        def _():
            def start(step, carry):
                to(k, step).start()
                return carry

            lax.fori_loop(1, XS * ZS, start, 0)
            betas[k] = beta_ref[...]
    for c in range(BLKS):
        pltpu.make_async_copy(x_hbm.at[pl.ds(c * PART, PART)], xbuf.at[pl.ds(c * PART, PART)], load_sem.at[c]).wait()
    for k in range(PENALTIES):
        @pl.when(samp != solver_of(k, core))
        def _():
            to(k, 1).wait_recv()
    wide_low[...] = jnp.zeros_like(wide_low)
    for k in range(PENALTIES):
        for t in range(TRAITS):
            row = 4 * t + k if k < 4 else 16 + t
            for j in range(4):
                piece = betas[k, 4 * j + t:4 * j + t + 1, :]
                coef_ref[PENALTIES * t + k:PENALTIES * t + k + 1, 128 * j:128 * j + 128] = piece
                wide_low[row:row + 1, 128 * j:128 * j + 128] = piece
    low = wide_low[...].astype(BF16)

    quarter = PART // 4

    def predict(owner, dst):
        part = xbuf[rows_at(owner, PART), :]
        values = lax.dot_general(low, part, NT, preferred_element_type=F32)
        dst[:, 0:PART] = values[0:16].astype(BF16)
        last = values[16:20]
        dst[:, PART:] = jnp.concatenate([last[:, quarter * q:quarter * q + quarter] for q in range(4)], 0).astype(BF16)

    def part_copy(step):
        owner = lax.rem(blk + step, BLKS)
        return pltpu.make_async_remote_copy(
            src_ref=stage.at[step], dst_ref=pall.at[blk], send_sem=psem.at[0, step], recv_sem=psem.at[1, step],
            device_id={"blk": owner}, device_id_type=MESH)

    def emit(step, carry):
        predict(lax.rem(blk + step, BLKS), stage.at[step])
        part_copy(step).start()
        return carry

    lax.fori_loop(1, BLKS, emit, 0)
    predict(blk, pall.at[blk])

    def landed(step, carry):
        part_copy(step).wait()
        return carry

    lax.fori_loop(1, BLKS, landed, 0)

    for k in range(PENALTIES):
        @pl.when(samp == solver_of(k, core))
        def _():
            def sent(step, carry):
                to(k, step).wait_send()
                return carry

            lax.fori_loop(1, XS * ZS, sent, 0)

    own = ph_ref[:, rows_at(blk, PART)].astype(F32)
    mains = [pall[b, :, 0:PART].astype(F32) for b in range(BLKS)]
    lasts = [pall[b, :, PART:].astype(F32) for b in range(BLKS)]
    by_trait = []
    for t in range(TRAITS):
        fifth = [jnp.concatenate([last[4 * q + t:4 * q + t + 1] for last in lasts], 0) for q in range(4)]
        pt = jnp.concatenate([main[4 * t:4 * t + 4] for main in mains] + [jnp.concatenate(fifth, 1)], 0)
        rows = jnp.concatenate([pt, own, jnp.zeros((4, PART), F32)], 0).astype(BF16)
        pt = jnp.concatenate([pt, jnp.zeros((24, PART), F32)], 0).astype(BF16)
        by_trait.append(pt)
        sums = lax.dot_general(rows, pt, NT, preferred_element_type=F32)
        lg[t] = jnp.concatenate([sums[0:24], sums[24:48]], 1)
    copies = []
    for step in range(1, BLKS):
        other = lax.rem(blk + step, BLKS)
        copies.append(send(lg.at[lax.div(other, 2)], ly.at[step - 1], ysem, step - 1, {"blk": other}))
    finish(copies)
    total = lg[y]
    for i in range(BLKS - 1):
        total = total + ly[i]
    ls[1] = total
    copies = []
    for step in range(1, XS):
        copies.append(send(ls.at[1], lx.at[step - 1], xsem, step - 1, along_x(x, z, step)[1]))
    finish(copies)
    total = ls[1]
    for i in range(XS - 1):
        total = total + lx[i]
    ls[2] = total
    copies = []
    for step in range(1, ZS):
        copies.append(send(ls.at[2], lz.at[step - 1], zsem, step - 1, along_z(x, z, step)[1]))
    finish(copies)
    total = ls[2]
    for i in range(ZS - 1):
        total = total + lz[i]
    total = total / SAMPLES
    full = jnp.concatenate([total, jnp.concatenate([total[:, 64:128], jnp.zeros((24, 64), F32)], 1)], 0)
    full = jnp.where(lax.broadcasted_iota(jnp.int32, full.shape, 1) < 64, full, 0.0)
    rows = [full[8 * i:8 * i + 8] + (jnp.where(lane == sub + 8 * i, level_penalty, 0.0) if i < 5 else 0.0) for i in range(6)]
    for t in range(5):
        rows = sweep(rows, t, lane, sub)
    mine = jnp.where(sub == y, -rows[5], 0.0)
    wt[...] = mine
    copies = []
    for step in range(1, 4):
        other = lax.rem(y + step, 4)
        copies.append(send(wt, wts.at[step - 1], wsem, step - 1, {"blk": other * 2 + core}))
    finish(copies)
    weights = mine + wts[0] + wts[1] + wts[2]
    wide = jnp.concatenate([jnp.where(sub == t, weights, 0.0)[:, 0:64] for t in range(TRAITS)], 1)
    w1 = wide.astype(BF16).astype(F32)
    w2 = (wide - w1).astype(BF16).astype(F32)
    w3 = wide - w1 - w2
    parts = jnp.concatenate([w1, w2, w3, jnp.zeros((8, 256), F32)], 0).astype(BF16)
    terms = lax.dot_general(parts, jnp.concatenate(by_trait, 0), NN, preferred_element_type=F32)
    pred_ref[...] = (terms[0:8] + terms[8:16] + terms[16:24])[0:4]


def level1(beta, phenotypes, genotypes):
    return pl.pallas_call(
        level1_kernel,
        out_shape=(jax.ShapeDtypeStruct((TRAITS, PART), F32), jax.ShapeDtypeStruct((TRAITS * PENALTIES, BLOCK), F32)),
        in_specs=[pl.BlockSpec(memory_space=VMEM), pl.BlockSpec(memory_space=VMEM), pl.BlockSpec(memory_space=pl.ANY)],
        out_specs=(pl.BlockSpec(memory_space=VMEM),) * 2,
        scratch_shapes=[
            VMEM((ROWS, BLOCK), BF16), VMEM((PENALTIES, 4 * TRAITS, 128), F32), VMEM((32, BLOCK), F32),
            VMEM((BLKS, 16, PART + PART // 4), BF16), VMEM((BLKS, 16, PART + PART // 4), BF16),
            VMEM((4, 24, 128), F32), VMEM((BLKS - 1, 24, 128), F32), VMEM((XS - 1, 24, 128), F32),
            VMEM((ZS - 1, 24, 128), F32), VMEM((3, 24, 128), F32), VMEM((8, 128), F32), VMEM((3, 8, 128), F32),
            pltpu.SemaphoreType.DMA((BLKS,)),
            pltpu.SemaphoreType.DMA((XS * ZS,)), pltpu.SemaphoreType.DMA((PENALTIES,)), dma(BLKS), dma(BLKS - 1), dma(XS - 1), dma(ZS - 1), dma(3),
        ],
        compiler_params=pltpu.CompilerParams(
            collective_id=1, has_side_effects=True, vmem_limit_bytes=57 << 20),
        name="level1",
    )(beta, phenotypes, genotypes)


def local(genotypes, phenotypes):
    sums = gram_sum(genotypes, phenotypes)
    beta = solve0(sums)
    return level1(beta, phenotypes, genotypes)


def solution(mesh):
    return jax.shard_map(
        local,
        mesh=mesh,
        in_specs=(P("samp", "blk"), P(None, "samp")),
        out_specs=(P(None, ("samp", "blk")), P(None, "blk")),
        check_vma=False,
    )
```

```python
import jax
import jax.numpy as jnp
from jax import lax
from jax.experimental import pallas as pl
from jax.experimental.pallas import tpu as pltpu
from jax.sharding import PartitionSpec as P

TRAITS = 4
PENALTIES = 5
SAMPLES = 262144
BLOCK = 512
XS, ZS, BLKS = 4, 8, 8
ridge_levels = (0.1, 0.4, 1.6, 6.4, 25.6)
level_penalty = 0.5

ROWS = SAMPLES // (XS * ZS)
PART = ROWS // BLKS
F32 = jnp.float32
BF16 = jnp.bfloat16
HI = lax.Precision.HIGHEST
NT = (((1,), (1,)), ((), ()))
NN = (((1,), (0,)), ((), ()))
MESH = pl.DeviceIdType.MESH
VMEM = pltpu.VMEM

CHUNK = 2048
A_ROWS = 1024
B_ROWS = 256
PACKED = A_ROWS + B_ROWS
OWNED = 40
USED = 1168
BELOW = {(1, 0): 0, (2, 0): 128, (3, 0): 256, (2, 1): 384, (3, 1): 512, (3, 2): 640}
TOP, CORNER, CROSS = 768, 1024, 1152

SOLVERS = ((0, 13), (9, 22), (18, 31), (27, 16), (4, 2))


def place():
    samp = lax.axis_index("samp")
    return lax.div(samp, ZS), lax.rem(samp, ZS)


def solver_of(k, core):
    first, second = SOLVERS[k]
    return first + core * (second - first)


def solves(samp, core):
    count = jnp.int32(0)
    for k in range(PENALTIES):
        count = count + jnp.where(samp == solver_of(k, core), jnp.int32(1), jnp.int32(0))
    return count


def along_x(x, z, step):
    other = lax.rem(x + step, XS)
    return other, {"samp": other * ZS + z}


def along_z(x, z, step):
    other = lax.rem(z + step, ZS)
    return other, {"samp": x * ZS + other}


def rows_at(index, size):
    return pl.ds(pl.multiple_of(index * size, size), size)


def send(src, dst, sems, slot, device):
    copy = pltpu.make_async_remote_copy(
        src_ref=src, dst_ref=dst, send_sem=sems.at[0, slot], recv_sem=sems.at[1, slot],
        device_id=device, device_id_type=MESH)
    copy.start()
    return copy


def finish(copies):
    for copy in copies:
        copy.wait()


def gram_sum(x_hbm, ph_ref, out_ref, xbuf, left, right, acc, ax, axs, az, bz, bzs, bx, mine,
                    load_sem, axr, azr, bzr, bxr, out_sem, in_sem):
    x, z = place()
    samp = lax.axis_index("samp")
    core = lax.rem(lax.axis_index("blk"), 2)
    chunks = ROWS // CHUNK
    for c in range(chunks):
        pltpu.make_async_copy(x_hbm.at[pl.ds(c * CHUNK, CHUNK)], xbuf.at[pl.ds(c * CHUNK, CHUNK)], load_sem.at[c]).start()
    barrier = pltpu.get_barrier_semaphore()
    for step in range(1, XS):
        pl.semaphore_signal(barrier, inc=1, device_id=along_x(x, z, step)[1], device_id_type=MESH)
    for step in range(1, ZS):
        pl.semaphore_signal(barrier, inc=1, device_id=along_z(x, z, step)[1], device_id_type=MESH)
    for k in range(PENALTIES):
        @pl.when(samp == solver_of(k, core))
        def _():
            def greet(step, carry):
                other = lax.rem(samp + step, XS * ZS)
                pl.semaphore_signal(barrier, inc=1, device_id={"samp": other}, device_id_type=MESH)
                return carry

            lax.fori_loop(1, XS * ZS, greet, 0)

    for step in range(1, BLKS):
        other = lax.rem(lax.axis_index("blk") + step, BLKS)
        pl.semaphore_signal(barrier, inc=1, device_id={"blk": other}, device_id_type=MESH)
    for k in range(PENALTIES):
        @pl.when(samp != solver_of(k, core))
        def _():
            pl.semaphore_signal(barrier, inc=1, device_id={"samp": solver_of(k, core)}, device_id_type=MESH)

    left[...] = jnp.zeros_like(left)
    right[...] = jnp.zeros_like(right)
    for c in range(chunks):
        span = pl.ds(c * CHUNK, CHUNK)
        pltpu.make_async_copy(x_hbm.at[span], xbuf.at[span], load_sem.at[c]).wait()
        values = xbuf[span, :]
        flipped = jnp.concatenate([values.T, ph_ref[:, span], jnp.zeros((12, CHUNK), BF16)], 0)
        left[...] += lax.dot_general(flipped, values[:, :256], NN, preferred_element_type=F32)
        right[...] += lax.dot_general(flipped[256:], values[:, 256:], NN, preferred_element_type=F32)

    def block(i, j, top=0, size=128):
        if j < 2:
            return left[128 * i + top:128 * i + top + size, 128 * j:128 * j + 128]
        return right[128 * i - 256 + top:128 * i - 256 + top + size, 128 * j - 256:128 * j - 128]

    for (i, j), row in BELOW.items():
        acc[row:row + 128, :] = block(i, j)
    for k in range(4):
        acc[TOP + 64 * k:TOP + 64 * k + 64, :] = block(k, k, 0, 64)
    for k in range(2):
        acc[CORNER + 64 * k:CORNER + 64 * k + 64, :] = jnp.concatenate(
            [block(2 * k, 2 * k, 64, 64)[:, 64:], block(2 * k + 1, 2 * k + 1, 64, 64)[:, 64:]], 1)
    acc[CROSS:CROSS + 8, :] = jnp.concatenate([left[512:516, 0:128], left[512:516, 128:256]], 0)
    acc[CROSS + 8:CROSS + 16, :] = jnp.concatenate([right[256:260, 0:128], right[256:260, 128:256]], 0)
    acc[USED:PACKED, :] = jnp.zeros((PACKED - USED, 128), F32)

    def b_rows(index):
        return pl.ds(pl.multiple_of(A_ROWS + index * 32, 32), 32)

    solving = solves(samp, core)
    pl.semaphore_wait(barrier, XS + ZS + BLKS - 3 + PENALTIES - solving + (XS * ZS - 1) * solving)
    a_out, b_out = [], []
    for step in range(1, ZS):
        other, device = along_z(x, z, step)
        b_out.append(send(acc.at[b_rows(other)], bz.at[step - 1], bzr, step - 1, device))
    for step in range(1, XS):
        other, device = along_x(x, z, step)
        a_out.append(send(acc.at[rows_at(other, 256)], ax.at[step - 1], axr, step - 1, device))
    finish(a_out)
    total = acc[rows_at(x, 256), :]
    for i in range(XS - 1):
        total = total + ax[i]
    axs[...] = total
    a_out = []
    for step in range(1, ZS):
        other, device = along_z(x, z, step)
        a_out.append(send(axs.at[rows_at(other, 32)], az.at[step - 1], azr, step - 1, device))
    finish(b_out)
    total = acc[b_rows(z), :]
    for i in range(ZS - 1):
        total = total + bz[i]
    bzs[...] = total
    b_out = []
    for step in range(1, XS):
        other, device = along_x(x, z, step)
        b_out.append(send(bzs.at[rows_at(other, 8)], bx.at[step - 1], bxr, step - 1, device))
    finish(b_out)
    total = bzs[rows_at(x, 8), :]
    for i in range(XS - 1):
        total = total + bx[i]
    mine[32:40, :] = total
    finish(a_out)
    total = axs[rows_at(z, 32), :]
    for i in range(ZS - 1):
        total = total + az[i]
    mine[0:32, :] = total

    def to(k, source):
        return pltpu.make_async_remote_copy(
            src_ref=mine, dst_ref=out_ref.at[rows_at(source, OWNED)], send_sem=out_sem.at[k], recv_sem=in_sem.at[source],
            device_id={"samp": solver_of(k, core)}, device_id_type=MESH)

    for k in range(PENALTIES):
        @pl.when(samp != solver_of(k, core))
        def _():
            to(k, samp).start()
    for k in range(PENALTIES):
        @pl.when(samp == solver_of(k, core))
        def _():
            out_ref[rows_at(samp, OWNED), :] = mine[...]

            def take(step, carry):
                to(k, lax.rem(samp + step, XS * ZS)).wait_recv()
                return carry

            lax.fori_loop(1, XS * ZS, take, 0)
    for k in range(PENALTIES):
        @pl.when(samp != solver_of(k, core))
        def _():
            to(k, samp).wait_send()


def dma(n):
    return pltpu.SemaphoreType.DMA((2, n))


def recip(d):
    r = pl.reciprocal(d, approx=True)
    r = r * (2.0 - d * r)
    return r


def tree(terms):
    while len(terms) > 1:
        terms = [terms[i] + terms[i + 1] for i in range(0, len(terms), 2)]
    return terms[0]


def sweep(rows, t, lane, sub):
    lo = 8 * t
    inside = (lane >= lo) & (lane < lo + 8)
    pivot_rows = rows[t]
    cols = [jnp.broadcast_to(pivot_rows[:, lo + j:lo + j + 1], (8, 128)) for j in range(8)]
    kept = jnp.where(inside, jnp.where(lane == sub + lo, 1.0, 0.0), pivot_rows)
    for p in range(8):
        col = cols[p]
        row = [jnp.broadcast_to(cols[j][p:p + 1, :], (8, 128)) for j in range(8)]
        r = recip(row[p])
        cols = [
            jnp.where(sub == p, r, -col * r) if j == p
            else jnp.where(sub == p, row[j] * r, cols[j] - (col * row[j]) * r)
            for j in range(8)
        ]
    new = tree([cols[j] * jnp.broadcast_to(kept[j:j + 1, :], (8, 128)) for j in range(8)])
    spread = [jnp.broadcast_to(new[j:j + 1, :], (8, 128)) for j in range(8)]
    out = []
    for i, group in enumerate(rows):
        if i == t:
            out.append(new)
        else:
            q = [jnp.broadcast_to(group[:, lo + j:lo + j + 1], (8, 128)) for j in range(8)]
            out.append(jnp.where(inside, 0.0, group) - tree([q[j] * spread[j] for j in range(8)]))
    return out


def iotas():
    shape = (8, 128)
    return lax.broadcasted_iota(jnp.int32, shape, 1), lax.broadcasted_iota(jnp.int32, shape, 0)


def solve0(g_ref, x_ref, a_ref, w_ref, inv_ref):
    lane, sub = iotas()
    samp = lax.axis_index("samp")
    core = lax.rem(lax.axis_index("blk"), 2)
    penalty = jnp.float32(ridge_levels[0])
    for k in range(1, PENALTIES):
        penalty = jnp.where(samp == solver_of(k, core), jnp.float32(ridge_levels[k]), penalty)

    def packed(row, count):
        pieces = []
        while count:
            if row < A_ROWS:
                owner, skip = row // 32, row % 32
                size = min(32 - skip, count)
                start = OWNED * owner + skip
            else:
                owner, skip = ((row - A_ROWS) % 32) // 8 * ZS + (row - A_ROWS) // 32, row % 8
                size = min(8 - skip, count)
                start = OWNED * owner + 32 + skip
            pieces.append(g_ref[start:start + size, :])
            row, count = row + size, count - size
        return (jnp.concatenate(pieces, 0) if len(pieces) > 1 else pieces[0]) / SAMPLES

    off = (0, 520, 912, 1176)
    for k in range(4):
        n = 512 - 128 * k
        upper = packed(TOP + 64 * k, 64)
        corner = packed(CORNER + 64 * (k // 2), 64)[:, 64 * (k % 2):64 * (k % 2) + 64]
        a_ref[off[k]:off[k] + 64, :] = upper
        a_ref[off[k] + 64:off[k] + 128, :] = jnp.concatenate([upper[:, 64:].T, corner], 1)
        for i in range(k + 1, 4):
            row = off[k] + 128 * (i - k)
            a_ref[row:row + 128, :] = packed(BELOW[i, k], 128)
        cross = packed(CROSS + 4 * k, 4)
        a_ref[off[k] + n:off[k] + n + 8, :] = jnp.concatenate([cross, jnp.zeros((4, 128), F32)], 0)
    for k in range(4):
        n = 512 - 128 * k
        rows = [a_ref[off[k] + 8 * i:off[k] + 8 * i + 8, :] + jnp.where(lane == sub + 8 * i, penalty, 0.0)
                for i in range(16)]
        for t in range(16):
            rows = sweep(rows, t, lane, sub)
        for i in range(16):
            inv_ref[8 * i:8 * i + 8, :] = rows[i]
        panel = a_ref[off[k] + 128:off[k] + n + 8, :]
        w = lax.dot_general(panel, inv_ref[...], NN, precision=HI, preferred_element_type=F32)
        w_ref[off[k]:off[k] + n - 120, :] = w
        for j in range(k + 1, 4):
            skip = 128 * (j - k - 1)
            change = lax.dot_general(panel[skip:, :], w[skip:skip + 128, :], NT, precision=HI, preferred_element_type=F32)
            a_ref[off[j]:off[j] + 520 - 128 * j, :] -= change
    parts = [None] * 4
    for k in (3, 2, 1, 0):
        n = 512 - 128 * k
        y = w_ref[off[k] + n - 128:off[k] + n - 120, :]
        if k < 3:
            later = jnp.concatenate(parts[k + 1:], 1)
            y = y - lax.dot_general(later, w_ref[off[k]:off[k] + n - 128, :], NN, precision=HI, preferred_element_type=F32)
        parts[k] = y
    x_ref[...] = jnp.concatenate([part[0:TRAITS] for part in parts], 0)


def level1(beta_ref, ph_ref, pred_ref, coef_ref, xbuf, betas, wide_low, stage, pall, lg, ly, lx, lz, ls, wt, wts,
           bsem, bget, psem, ysem, xsem, zsem, wsem):
    x, z = place()
    blk = lax.axis_index("blk")
    y, core = lax.div(blk, 2), lax.rem(blk, 2)
    lane, sub = iotas()
    samp = lax.axis_index("samp")
    def to(k, step):
        other = lax.rem(solver_of(k, core) + step, XS * ZS)
        return pltpu.make_async_remote_copy(
            src_ref=beta_ref, dst_ref=betas.at[k], send_sem=bsem.at[step], recv_sem=bget.at[k],
            device_id={"samp": other}, device_id_type=MESH)

    for k in range(PENALTIES):
        @pl.when(samp == solver_of(k, core))
        def _():
            def start(step, carry):
                to(k, step).start()
                return carry

            lax.fori_loop(1, XS * ZS, start, 0)
            betas[k] = beta_ref[...]
    for k in range(PENALTIES):
        @pl.when(samp != solver_of(k, core))
        def _():
            to(k, 1).wait_recv()
    wide_low[...] = jnp.zeros_like(wide_low)
    for k in range(PENALTIES):
        for t in range(TRAITS):
            row = 4 * t + k if k < 4 else 16 + t
            for j in range(4):
                piece = betas[k, 4 * j + t:4 * j + t + 1, :]
                coef_ref[PENALTIES * t + k:PENALTIES * t + k + 1, 128 * j:128 * j + 128] = piece
                wide_low[row:row + 1, 128 * j:128 * j + 128] = piece
    low = wide_low[...].astype(BF16)

    quarter = PART // 4

    def predict(owner, dst):
        part = xbuf[rows_at(owner, PART), :]
        values = lax.dot_general(low, part, NT, preferred_element_type=F32)
        dst[:, 0:PART] = values[0:16].astype(BF16)
        last = values[16:20]
        dst[:, PART:] = jnp.concatenate([last[:, quarter * q:quarter * q + quarter] for q in range(4)], 0).astype(BF16)

    def part_copy(step):
        owner = lax.rem(blk + step, BLKS)
        return pltpu.make_async_remote_copy(
            src_ref=stage.at[step], dst_ref=pall.at[blk], send_sem=psem.at[0, step], recv_sem=psem.at[1, step],
            device_id={"blk": owner}, device_id_type=MESH)

    def emit(step, carry):
        predict(lax.rem(blk + step, BLKS), stage.at[step])
        part_copy(step).start()
        return carry

    lax.fori_loop(1, BLKS, emit, 0)
    predict(blk, pall.at[blk])

    def landed(step, carry):
        part_copy(step).wait()
        return carry

    lax.fori_loop(1, BLKS, landed, 0)

    for k in range(PENALTIES):
        @pl.when(samp == solver_of(k, core))
        def _():
            def sent(step, carry):
                to(k, step).wait_send()
                return carry

            lax.fori_loop(1, XS * ZS, sent, 0)

    own = ph_ref[:, rows_at(blk, PART)].astype(F32)
    mains = [pall[b, :, 0:PART].astype(F32) for b in range(BLKS)]
    lasts = [pall[b, :, PART:].astype(F32) for b in range(BLKS)]
    by_trait = []
    for t in range(TRAITS):
        fifth = [jnp.concatenate([last[4 * q + t:4 * q + t + 1] for last in lasts], 0) for q in range(4)]
        pt = jnp.concatenate([main[4 * t:4 * t + 4] for main in mains] + [jnp.concatenate(fifth, 1)], 0)
        rows = jnp.concatenate([pt, own, jnp.zeros((4, PART), F32)], 0).astype(BF16)
        pt = jnp.concatenate([pt, jnp.zeros((24, PART), F32)], 0).astype(BF16)
        by_trait.append(pt)
        sums = lax.dot_general(rows, pt, NT, preferred_element_type=F32)
        lg[t] = jnp.concatenate([sums[0:24], sums[24:48]], 1)
    copies = []
    for step in range(1, BLKS):
        other = lax.rem(blk + step, BLKS)
        copies.append(send(lg.at[lax.div(other, 2)], ly.at[step - 1], ysem, step - 1, {"blk": other}))
    finish(copies)
    total = lg[y]
    for i in range(BLKS - 1):
        total = total + ly[i]
    ls[1] = total
    copies = []
    for step in range(1, XS):
        copies.append(send(ls.at[1], lx.at[step - 1], xsem, step - 1, along_x(x, z, step)[1]))
    finish(copies)
    total = ls[1]
    for i in range(XS - 1):
        total = total + lx[i]
    ls[2] = total
    copies = []
    for step in range(1, ZS):
        copies.append(send(ls.at[2], lz.at[step - 1], zsem, step - 1, along_z(x, z, step)[1]))
    finish(copies)
    total = ls[2]
    for i in range(ZS - 1):
        total = total + lz[i]
    total = total / SAMPLES
    full = jnp.concatenate([total, jnp.concatenate([total[:, 64:128], jnp.zeros((24, 64), F32)], 1)], 0)
    full = jnp.where(lax.broadcasted_iota(jnp.int32, full.shape, 1) < 64, full, 0.0)
    rows = [full[8 * i:8 * i + 8] + (jnp.where(lane == sub + 8 * i, level_penalty, 0.0) if i < 5 else 0.0) for i in range(6)]
    for t in range(5):
        rows = sweep(rows, t, lane, sub)
    mine = jnp.where(sub == y, -rows[5], 0.0)
    wt[...] = mine
    copies = []
    for step in range(1, 4):
        other = lax.rem(y + step, 4)
        copies.append(send(wt, wts.at[step - 1], wsem, step - 1, {"blk": other * 2 + core}))
    finish(copies)
    weights = mine + wts[0] + wts[1] + wts[2]
    wide = jnp.concatenate([jnp.where(sub == t, weights, 0.0)[:, 0:64] for t in range(TRAITS)], 1)
    w1 = wide.astype(BF16).astype(F32)
    w2 = (wide - w1).astype(BF16).astype(F32)
    w3 = wide - w1 - w2
    parts = jnp.concatenate([w1, w2, w3, jnp.zeros((8, 256), F32)], 0).astype(BF16)
    terms = lax.dot_general(parts, jnp.concatenate(by_trait, 0), NN, preferred_element_type=F32)
    pred_ref[...] = (terms[0:8] + terms[8:16] + terms[16:24])[0:4]


def ridge_kernel(x_hbm, ph_ref, pred_ref, coef_ref, xbuf, sums, beta, *scratch):
    samp = lax.axis_index("samp")
    core = lax.rem(lax.axis_index("blk"), 2)
    gram_sum(x_hbm, ph_ref, sums, xbuf, *scratch[:17])

    @pl.when(solves(samp, core) == 1)
    def _():
        solve0(sums, beta, *scratch[17:20])

    level1(beta, ph_ref, pred_ref, coef_ref, xbuf, *scratch[20:])


def local(genotypes, phenotypes):
    x1, z1 = XS - 1, ZS - 1
    sems = pltpu.SemaphoreType.DMA
    gram_scratch = [
        VMEM((528, 256), F32), VMEM((272, 256), F32), VMEM((PACKED, 128), F32),
        VMEM((x1, 256, 128), F32), VMEM((256, 128), F32), VMEM((z1, 32, 128), F32),
        VMEM((z1, 32, 128), F32), VMEM((32, 128), F32), VMEM((x1, 8, 128), F32), VMEM((OWNED, 128), F32),
        sems((ROWS // CHUNK,)), dma(x1), dma(z1), dma(z1), dma(x1), sems((PENALTIES,)), sems((XS * ZS,)),
    ]
    solve_scratch = [VMEM((1312, 128), F32), VMEM((1312, 128), F32), VMEM((128, 128), F32)]
    level1_scratch = [
        VMEM((PENALTIES, 4 * TRAITS, 128), F32), VMEM((32, BLOCK), F32),
        VMEM((BLKS, 16, PART + PART // 4), BF16), VMEM((BLKS, 16, PART + PART // 4), BF16),
        VMEM((4, 24, 128), F32), VMEM((BLKS - 1, 24, 128), F32), VMEM((x1, 24, 128), F32),
        VMEM((z1, 24, 128), F32), VMEM((3, 24, 128), F32), VMEM((8, 128), F32), VMEM((3, 8, 128), F32),
        sems((XS * ZS,)), sems((PENALTIES,)), dma(BLKS), dma(BLKS - 1), dma(x1), dma(z1), dma(3),
    ]
    return pl.pallas_call(
        ridge_kernel,
        out_shape=(jax.ShapeDtypeStruct((TRAITS, PART), F32), jax.ShapeDtypeStruct((TRAITS * PENALTIES, BLOCK), F32)),
        in_specs=[pl.BlockSpec(memory_space=pl.ANY), pl.BlockSpec(memory_space=VMEM)],
        out_specs=(pl.BlockSpec(memory_space=VMEM),) * 2,
        scratch_shapes=[
            VMEM((ROWS, BLOCK), BF16), VMEM((XS * ZS * OWNED, 128), F32), VMEM((4 * TRAITS, 128), F32),
            *gram_scratch, *solve_scratch, *level1_scratch,
        ],
        compiler_params=pltpu.CompilerParams(
            collective_id=0, has_side_effects=True, vmem_limit_bytes=57 << 20),
        name="ridge",
    )(genotypes, phenotypes)


def solution(mesh):
    return jax.shard_map(
        local,
        mesh=mesh,
        in_specs=(P("samp", "blk"), P(None, "samp")),
        out_specs=(P(None, ("samp", "blk")), P(None, "blk")),
        check_vma=False,
    )
```

```python
import jax
import jax.numpy as jnp
from jax import lax
from jax.experimental import pallas as pl
from jax.experimental.pallas import tpu as pltpu
from jax.sharding import PartitionSpec as P

TRAITS = 4
PENALTIES = 5
SAMPLES = 262144
BLOCK = 512
XS, ZS, BLKS = 4, 8, 8
ridge_levels = (0.1, 0.4, 1.6, 6.4, 25.6)
level_penalty = 0.5

ROWS = SAMPLES // (XS * ZS)
PART = ROWS // BLKS
F32 = jnp.float32
BF16 = jnp.bfloat16
HI = lax.Precision.HIGHEST
NT = (((1,), (1,)), ((), ()))
NN = (((1,), (0,)), ((), ()))
MESH = pl.DeviceIdType.MESH
VMEM = pltpu.VMEM

CHUNK = 2048
A_ROWS = 1024
B_ROWS = 256
PACKED = A_ROWS + B_ROWS
OWNED = 40
X_STEPS = (2, 1, 3)
Z_STEPS = (4, 3, 5, 2, 6, 1, 7)
FAR_FIRST = sorted(
    ((dx, dz) for dx in range(XS) for dz in range(ZS) if dx or dz),
    key=lambda step: -(min(step[0], XS - step[0]) + min(step[1], ZS - step[1])))
USED = 1168
BELOW = {(1, 0): 0, (2, 0): 128, (3, 0): 256, (2, 1): 384, (3, 1): 512, (3, 2): 640}
TOP, CORNER, CROSS = 768, 1024, 1152

SOLVERS = ((0, 13), (9, 22), (18, 31), (27, 16), (4, 2))


def place():
    samp = lax.axis_index("samp")
    return lax.div(samp, ZS), lax.rem(samp, ZS)


def solver_of(k, core):
    first, second = SOLVERS[k]
    return first + core * (second - first)


def solves(samp, core):
    count = jnp.int32(0)
    for k in range(PENALTIES):
        count = count + jnp.where(samp == solver_of(k, core), jnp.int32(1), jnp.int32(0))
    return count


def along_x(x, z, step):
    other = lax.rem(x + step, XS)
    return other, {"samp": other * ZS + z}


def along_z(x, z, step):
    other = lax.rem(z + step, ZS)
    return other, {"samp": x * ZS + other}


def rows_at(index, size):
    return pl.ds(pl.multiple_of(index * size, size), size)


def send(src, dst, sems, slot, device):
    copy = pltpu.make_async_remote_copy(
        src_ref=src, dst_ref=dst, send_sem=sems.at[0, slot], recv_sem=sems.at[1, slot],
        device_id=device, device_id_type=MESH)
    copy.start()
    return copy


def finish(copies):
    for copy in copies:
        copy.wait()


def gram_sum(x_hbm, ph_ref, out_ref, xbuf, left, right, acc, ax, axs, az, bz, bzs, bx, mine,
                    load_sem, axr, azr, bzr, bxr, out_sem, in_sem):
    x, z = place()
    samp = lax.axis_index("samp")
    core = lax.rem(lax.axis_index("blk"), 2)
    chunks = ROWS // CHUNK
    for c in range(chunks):
        pltpu.make_async_copy(x_hbm.at[pl.ds(c * CHUNK, CHUNK)], xbuf.at[pl.ds(c * CHUNK, CHUNK)], load_sem.at[c]).start()
    barrier = pltpu.get_barrier_semaphore()
    for step in range(1, XS):
        pl.semaphore_signal(barrier, inc=1, device_id=along_x(x, z, step)[1], device_id_type=MESH)
    for step in range(1, ZS):
        pl.semaphore_signal(barrier, inc=1, device_id=along_z(x, z, step)[1], device_id_type=MESH)
    for k in range(PENALTIES):
        @pl.when(samp == solver_of(k, core))
        def _():
            def greet(step, carry):
                other = lax.rem(samp + step, XS * ZS)
                pl.semaphore_signal(barrier, inc=1, device_id={"samp": other}, device_id_type=MESH)
                return carry

            lax.fori_loop(1, XS * ZS, greet, 0)

    for step in range(1, BLKS):
        other = lax.rem(lax.axis_index("blk") + step, BLKS)
        pl.semaphore_signal(barrier, inc=1, device_id={"blk": other}, device_id_type=MESH)
    for k in range(PENALTIES):
        @pl.when(samp != solver_of(k, core))
        def _():
            pl.semaphore_signal(barrier, inc=1, device_id={"samp": solver_of(k, core)}, device_id_type=MESH)

    left[...] = jnp.zeros_like(left)
    right[...] = jnp.zeros_like(right)
    for c in range(chunks):
        span = pl.ds(c * CHUNK, CHUNK)
        pltpu.make_async_copy(x_hbm.at[span], xbuf.at[span], load_sem.at[c]).wait()
        values = xbuf[span, :]
        flipped = jnp.concatenate([values.T, ph_ref[:, span], jnp.zeros((12, CHUNK), BF16)], 0)
        left[...] += lax.dot_general(flipped, values[:, :256], NN, preferred_element_type=F32)
        right[...] += lax.dot_general(flipped[256:], values[:, 256:], NN, preferred_element_type=F32)

    def block(i, j, top=0, size=128):
        if j < 2:
            return left[128 * i + top:128 * i + top + size, 128 * j:128 * j + 128]
        return right[128 * i - 256 + top:128 * i - 256 + top + size, 128 * j - 256:128 * j - 128]

    for (i, j), row in BELOW.items():
        acc[row:row + 128, :] = block(i, j)
    for k in range(4):
        acc[TOP + 64 * k:TOP + 64 * k + 64, :] = block(k, k, 0, 64)
    for k in range(2):
        acc[CORNER + 64 * k:CORNER + 64 * k + 64, :] = jnp.concatenate(
            [block(2 * k, 2 * k, 64, 64)[:, 64:], block(2 * k + 1, 2 * k + 1, 64, 64)[:, 64:]], 1)
    acc[CROSS:CROSS + 8, :] = jnp.concatenate([left[512:516, 0:128], left[512:516, 128:256]], 0)
    acc[CROSS + 8:CROSS + 16, :] = jnp.concatenate([right[256:260, 0:128], right[256:260, 128:256]], 0)
    acc[USED:PACKED, :] = jnp.zeros((PACKED - USED, 128), F32)

    def b_rows(index):
        return pl.ds(pl.multiple_of(A_ROWS + index * 32, 32), 32)

    solving = solves(samp, core)
    pl.semaphore_wait(barrier, XS + ZS + BLKS - 3 + PENALTIES - solving + (XS * ZS - 1) * solving)
    a_out, b_out = [], []
    for step in Z_STEPS:
        other, device = along_z(x, z, step)
        b_out.append(send(acc.at[b_rows(other)], bz.at[step - 1], bzr, step - 1, device))
    for step in X_STEPS:
        other, device = along_x(x, z, step)
        a_out.append(send(acc.at[rows_at(other, 256)], ax.at[step - 1], axr, step - 1, device))
    finish(a_out)
    total = acc[rows_at(x, 256), :]
    for i in range(XS - 1):
        total = total + ax[i]
    axs[...] = total
    a_out = []
    for step in Z_STEPS:
        other, device = along_z(x, z, step)
        a_out.append(send(axs.at[rows_at(other, 32)], az.at[step - 1], azr, step - 1, device))
    finish(b_out)
    total = acc[b_rows(z), :]
    for i in range(ZS - 1):
        total = total + bz[i]
    bzs[...] = total
    b_out = []
    for step in X_STEPS:
        other, device = along_x(x, z, step)
        b_out.append(send(bzs.at[rows_at(other, 8)], bx.at[step - 1], bxr, step - 1, device))
    finish(b_out)
    total = bzs[rows_at(x, 8), :]
    for i in range(XS - 1):
        total = total + bx[i]
    mine[32:40, :] = total
    finish(a_out)
    total = axs[rows_at(z, 32), :]
    for i in range(ZS - 1):
        total = total + az[i]
    mine[0:32, :] = total

    def to(k, source):
        return pltpu.make_async_remote_copy(
            src_ref=mine, dst_ref=out_ref.at[rows_at(source, OWNED)], send_sem=out_sem.at[k], recv_sem=in_sem.at[source],
            device_id={"samp": solver_of(k, core)}, device_id_type=MESH)

    for k in range(PENALTIES):
        @pl.when(samp != solver_of(k, core))
        def _():
            to(k, samp).start()
    for k in range(PENALTIES):
        @pl.when(samp == solver_of(k, core))
        def _():
            out_ref[rows_at(samp, OWNED), :] = mine[...]

            def take(step, carry):
                to(k, lax.rem(samp + step, XS * ZS)).wait_recv()
                return carry

            lax.fori_loop(1, XS * ZS, take, 0)
    for k in range(PENALTIES):
        @pl.when(samp != solver_of(k, core))
        def _():
            to(k, samp).wait_send()


def dma(n):
    return pltpu.SemaphoreType.DMA((2, n))


def recip(d):
    r = pl.reciprocal(d, approx=True)
    r = r * (2.0 - d * r)
    return r


def tree(terms):
    while len(terms) > 1:
        terms = [terms[i] + terms[i + 1] for i in range(0, len(terms), 2)]
    return terms[0]


def sweep(rows, t, lane, sub):
    lo = 8 * t
    inside = (lane >= lo) & (lane < lo + 8)
    pivot_rows = rows[t]
    cols = [jnp.broadcast_to(pivot_rows[:, lo + j:lo + j + 1], (8, 128)) for j in range(8)]
    kept = jnp.where(inside, jnp.where(lane == sub + lo, 1.0, 0.0), pivot_rows)
    for p in range(8):
        col = cols[p]
        row = [jnp.broadcast_to(cols[j][p:p + 1, :], (8, 128)) for j in range(8)]
        r = recip(row[p])
        cols = [
            jnp.where(sub == p, r, -col * r) if j == p
            else jnp.where(sub == p, row[j] * r, cols[j] - (col * row[j]) * r)
            for j in range(8)
        ]
    new = tree([cols[j] * jnp.broadcast_to(kept[j:j + 1, :], (8, 128)) for j in range(8)])
    spread = [jnp.broadcast_to(new[j:j + 1, :], (8, 128)) for j in range(8)]
    out = []
    for i, group in enumerate(rows):
        if i == t:
            out.append(new)
        else:
            q = [jnp.broadcast_to(group[:, lo + j:lo + j + 1], (8, 128)) for j in range(8)]
            out.append(jnp.where(inside, 0.0, group) - tree([q[j] * spread[j] for j in range(8)]))
    return out


def iotas():
    shape = (8, 128)
    return lax.broadcasted_iota(jnp.int32, shape, 1), lax.broadcasted_iota(jnp.int32, shape, 0)


def solve0(g_ref, x_ref, a_ref, w_ref, inv_ref):
    lane, sub = iotas()
    samp = lax.axis_index("samp")
    core = lax.rem(lax.axis_index("blk"), 2)
    penalty = jnp.float32(ridge_levels[0])
    for k in range(1, PENALTIES):
        penalty = jnp.where(samp == solver_of(k, core), jnp.float32(ridge_levels[k]), penalty)

    def packed(row, count):
        pieces = []
        while count:
            if row < A_ROWS:
                owner, skip = row // 32, row % 32
                size = min(32 - skip, count)
                start = OWNED * owner + skip
            else:
                owner, skip = ((row - A_ROWS) % 32) // 8 * ZS + (row - A_ROWS) // 32, row % 8
                size = min(8 - skip, count)
                start = OWNED * owner + 32 + skip
            pieces.append(g_ref[start:start + size, :])
            row, count = row + size, count - size
        return (jnp.concatenate(pieces, 0) if len(pieces) > 1 else pieces[0]) / SAMPLES

    off = (0, 520, 912, 1176)
    for k in range(4):
        n = 512 - 128 * k
        upper = packed(TOP + 64 * k, 64)
        corner = packed(CORNER + 64 * (k // 2), 64)[:, 64 * (k % 2):64 * (k % 2) + 64]
        a_ref[off[k]:off[k] + 64, :] = upper
        a_ref[off[k] + 64:off[k] + 128, :] = jnp.concatenate([upper[:, 64:].T, corner], 1)
        for i in range(k + 1, 4):
            row = off[k] + 128 * (i - k)
            a_ref[row:row + 128, :] = packed(BELOW[i, k], 128)
        cross = packed(CROSS + 4 * k, 4)
        a_ref[off[k] + n:off[k] + n + 8, :] = jnp.concatenate([cross, jnp.zeros((4, 128), F32)], 0)
    for k in range(4):
        n = 512 - 128 * k
        rows = [a_ref[off[k] + 8 * i:off[k] + 8 * i + 8, :] + jnp.where(lane == sub + 8 * i, penalty, 0.0)
                for i in range(16)]
        for t in range(16):
            rows = sweep(rows, t, lane, sub)
        for i in range(16):
            inv_ref[8 * i:8 * i + 8, :] = rows[i]
        panel = a_ref[off[k] + 128:off[k] + n + 8, :]
        w = lax.dot_general(panel, inv_ref[...], NN, precision=HI, preferred_element_type=F32)
        w_ref[off[k]:off[k] + n - 120, :] = w
        for j in range(k + 1, 4):
            skip = 128 * (j - k - 1)
            change = lax.dot_general(panel[skip:, :], w[skip:skip + 128, :], NT, precision=HI, preferred_element_type=F32)
            a_ref[off[j]:off[j] + 520 - 128 * j, :] -= change
    parts = [None] * 4
    for k in (3, 2, 1, 0):
        n = 512 - 128 * k
        y = w_ref[off[k] + n - 128:off[k] + n - 120, :]
        if k < 3:
            later = jnp.concatenate(parts[k + 1:], 1)
            y = y - lax.dot_general(later, w_ref[off[k]:off[k] + n - 128, :], NN, precision=HI, preferred_element_type=F32)
        parts[k] = y
    x_ref[...] = jnp.concatenate([part[0:TRAITS] for part in parts], 0)


def level1(beta_ref, ph_ref, pred_ref, coef_ref, xbuf, betas, wide_low, stage, pall, lg, ly, lx, lz, ls, wt, wts,
           bsem, bget, psem, ysem, xsem, zsem, wsem):
    x, z = place()
    blk = lax.axis_index("blk")
    y, core = lax.div(blk, 2), lax.rem(blk, 2)
    lane, sub = iotas()
    samp = lax.axis_index("samp")
    which = jnp.int32(0)
    for k in range(1, PENALTIES):
        which = which + jnp.where(samp == solver_of(k, core), jnp.int32(k), jnp.int32(0))
    solving = solves(samp, core)

    def to(k, dx, dz):
        other = lax.rem(x + dx, XS) * ZS + lax.rem(z + dz, ZS)
        return pltpu.make_async_remote_copy(
            src_ref=beta_ref, dst_ref=betas.at[k], send_sem=bsem.at[dx * ZS + dz], recv_sem=bget.at[k],
            device_id={"samp": other}, device_id_type=MESH)

    @pl.when(solving == 1)
    def _():
        for dx, dz in FAR_FIRST:
            to(which, dx, dz).start()
        betas[which] = beta_ref[...]

    for k in range(PENALTIES):
        @pl.when(samp != solver_of(k, core))
        def _():
            to(k, 0, 1).wait_recv()
    wide_low[...] = jnp.zeros_like(wide_low)
    for k in range(PENALTIES):
        for t in range(TRAITS):
            row = 4 * t + k if k < 4 else 16 + t
            for j in range(4):
                piece = betas[k, 4 * j + t:4 * j + t + 1, :]
                coef_ref[PENALTIES * t + k:PENALTIES * t + k + 1, 128 * j:128 * j + 128] = piece
                wide_low[row:row + 1, 128 * j:128 * j + 128] = piece
    low = wide_low[...].astype(BF16)

    quarter = PART // 4

    def predict(owner, dst):
        part = xbuf[rows_at(owner, PART), :]
        values = lax.dot_general(low, part, NT, preferred_element_type=F32)
        dst[:, 0:PART] = values[0:16].astype(BF16)
        last = values[16:20]
        dst[:, PART:] = jnp.concatenate([last[:, quarter * q:quarter * q + quarter] for q in range(4)], 0).astype(BF16)

    def part_copy(step):
        owner = lax.rem(blk + step, BLKS)
        return pltpu.make_async_remote_copy(
            src_ref=stage.at[step], dst_ref=pall.at[blk], send_sem=psem.at[0, step], recv_sem=psem.at[1, step],
            device_id={"blk": owner}, device_id_type=MESH)

    def emit(step, carry):
        predict(lax.rem(blk + step, BLKS), stage.at[step])
        part_copy(step).start()
        return carry

    lax.fori_loop(1, BLKS, emit, 0)
    predict(blk, pall.at[blk])

    def landed(step, carry):
        part_copy(step).wait()
        return carry

    lax.fori_loop(1, BLKS, landed, 0)

    @pl.when(solving == 1)
    def _():
        for dx, dz in FAR_FIRST:
            to(which, dx, dz).wait_send()

    own = ph_ref[:, rows_at(blk, PART)].astype(F32)
    mains = [pall[b, :, 0:PART].astype(F32) for b in range(BLKS)]
    lasts = [pall[b, :, PART:].astype(F32) for b in range(BLKS)]
    by_trait = []
    for t in range(TRAITS):
        fifth = [jnp.concatenate([last[4 * q + t:4 * q + t + 1] for last in lasts], 0) for q in range(4)]
        pt = jnp.concatenate([main[4 * t:4 * t + 4] for main in mains] + [jnp.concatenate(fifth, 1)], 0)
        rows = jnp.concatenate([pt, own, jnp.zeros((4, PART), F32)], 0).astype(BF16)
        pt = jnp.concatenate([pt, jnp.zeros((24, PART), F32)], 0).astype(BF16)
        by_trait.append(pt)
        sums = lax.dot_general(rows, pt, NT, preferred_element_type=F32)
        lg[t] = jnp.concatenate([sums[0:24], sums[24:48]], 1)
    copies = []
    for step in range(1, BLKS):
        other = lax.rem(blk + step, BLKS)
        copies.append(send(lg.at[lax.div(other, 2)], ly.at[step - 1], ysem, step - 1, {"blk": other}))
    finish(copies)
    total = lg[y]
    for i in range(BLKS - 1):
        total = total + ly[i]
    ls[1] = total
    copies = []
    for step in X_STEPS:
        copies.append(send(ls.at[1], lx.at[step - 1], xsem, step - 1, along_x(x, z, step)[1]))
    finish(copies)
    total = ls[1]
    for i in range(XS - 1):
        total = total + lx[i]
    ls[2] = total
    copies = []
    for step in Z_STEPS:
        copies.append(send(ls.at[2], lz.at[step - 1], zsem, step - 1, along_z(x, z, step)[1]))
    finish(copies)
    total = ls[2]
    for i in range(ZS - 1):
        total = total + lz[i]
    total = total / SAMPLES
    full = jnp.concatenate([total, jnp.concatenate([total[:, 64:128], jnp.zeros((24, 64), F32)], 1)], 0)
    full = jnp.where(lax.broadcasted_iota(jnp.int32, full.shape, 1) < 64, full, 0.0)
    rows = [full[8 * i:8 * i + 8] + (jnp.where(lane == sub + 8 * i, level_penalty, 0.0) if i < 5 else 0.0) for i in range(6)]
    for t in range(5):
        rows = sweep(rows, t, lane, sub)
    mine = jnp.where(sub == y, -rows[5], 0.0)
    wt[...] = mine
    copies = []
    for step in range(1, 4):
        other = lax.rem(y + step, 4)
        copies.append(send(wt, wts.at[step - 1], wsem, step - 1, {"blk": other * 2 + core}))
    finish(copies)
    weights = mine + wts[0] + wts[1] + wts[2]
    wide = jnp.concatenate([jnp.where(sub == t, weights, 0.0)[:, 0:64] for t in range(TRAITS)], 1)
    w1 = wide.astype(BF16).astype(F32)
    w2 = (wide - w1).astype(BF16).astype(F32)
    w3 = wide - w1 - w2
    parts = jnp.concatenate([w1, w2, w3, jnp.zeros((8, 256), F32)], 0).astype(BF16)
    terms = lax.dot_general(parts, jnp.concatenate(by_trait, 0), NN, preferred_element_type=F32)
    pred_ref[...] = (terms[0:8] + terms[8:16] + terms[16:24])[0:4]


def ridge_kernel(x_hbm, ph_ref, pred_ref, coef_ref, xbuf, sums, beta, *scratch):
    samp = lax.axis_index("samp")
    core = lax.rem(lax.axis_index("blk"), 2)
    gram_sum(x_hbm, ph_ref, sums, xbuf, *scratch[:17])

    @pl.when(solves(samp, core) == 1)
    def _():
        solve0(sums, beta, *scratch[17:20])

    level1(beta, ph_ref, pred_ref, coef_ref, xbuf, *scratch[20:])


def local(genotypes, phenotypes):
    x1, z1 = XS - 1, ZS - 1
    sems = pltpu.SemaphoreType.DMA
    gram_scratch = [
        VMEM((528, 256), F32), VMEM((272, 256), F32), VMEM((PACKED, 128), F32),
        VMEM((x1, 256, 128), F32), VMEM((256, 128), F32), VMEM((z1, 32, 128), F32),
        VMEM((z1, 32, 128), F32), VMEM((32, 128), F32), VMEM((x1, 8, 128), F32), VMEM((OWNED, 128), F32),
        sems((ROWS // CHUNK,)), dma(x1), dma(z1), dma(z1), dma(x1), sems((PENALTIES,)), sems((XS * ZS,)),
    ]
    solve_scratch = [VMEM((1312, 128), F32), VMEM((1312, 128), F32), VMEM((128, 128), F32)]
    level1_scratch = [
        VMEM((PENALTIES, 4 * TRAITS, 128), F32), VMEM((32, BLOCK), F32),
        VMEM((BLKS, 16, PART + PART // 4), BF16), VMEM((BLKS, 16, PART + PART // 4), BF16),
        VMEM((4, 24, 128), F32), VMEM((BLKS - 1, 24, 128), F32), VMEM((x1, 24, 128), F32),
        VMEM((z1, 24, 128), F32), VMEM((3, 24, 128), F32), VMEM((8, 128), F32), VMEM((3, 8, 128), F32),
        sems((XS * ZS,)), sems((PENALTIES,)), dma(BLKS), dma(BLKS - 1), dma(x1), dma(z1), dma(3),
    ]
    return pl.pallas_call(
        ridge_kernel,
        out_shape=(jax.ShapeDtypeStruct((TRAITS, PART), F32), jax.ShapeDtypeStruct((TRAITS * PENALTIES, BLOCK), F32)),
        in_specs=[pl.BlockSpec(memory_space=pl.ANY), pl.BlockSpec(memory_space=VMEM)],
        out_specs=(pl.BlockSpec(memory_space=VMEM),) * 2,
        scratch_shapes=[
            VMEM((ROWS, BLOCK), BF16), VMEM((XS * ZS * OWNED, 128), F32), VMEM((4 * TRAITS, 128), F32),
            *gram_scratch, *solve_scratch, *level1_scratch,
        ],
        compiler_params=pltpu.CompilerParams(
            collective_id=0, has_side_effects=True, vmem_limit_bytes=50 << 20),
        name="ridge",
    )(genotypes, phenotypes)


def solution(mesh):
    return jax.shard_map(
        local,
        mesh=mesh,
        in_specs=(P("samp", "blk"), P(None, "samp")),
        out_specs=(P(None, ("samp", "blk")), P(None, "blk")),
        check_vma=False,
    )
```
